128 devices in a mesh: src: 32 (over x, y, core), tgt: 4 (over z).
Axes of the slice: x: 4, y: 4, z: 4, core: 2. Of those that a mesh axis runs over, the one named last changes fastest.
Arguments:
- source_embed: bfloat16 [65536, 768], P('src'), may hold values from -5 to 5
- target_embed: bfloat16 [8192, 768], P('tgt'), may hold values from -5 to 5
- source_potential: float32 [65536], P('src'), may hold values from -7 to -4
- target_potential: float32 [8192], replicated, may hold values from -5.5 to -3.5
- active_blocks: int32 [256, 24], P('src'), may hold values from 0 to 31, as said below
- active_count: int32 [256], P('src'), may hold values from 1 to 24, as said below
Outputs:
- grad_source: bfloat16 [65536, 768], P('src', 'tgt')
- grad_target: bfloat16 [8192, 768], P('tgt')
The draws below stay inside these ranges and needn't reach their ends.
Inputs may be any that keep to these rules, and one draw needn't show every extreme that they name: `active_blocks`: each block's 24 entries are distinct target block ids; only the first active_count entries are used. Some source block lists all 24. `active_count`: counts differ strongly between source blocks and between devices of src; some block has exactly 24.
All inputs are finite; a program needn't handle non-finite values.
Results may differ from the reference program's by a relative error of at most 0.005.
Values may be sent and summed in bfloat16 or wider, within the bound.
A program may use at most 128 MiB of HBM per device.

```python
import math
import jax
import jax.numpy as jnp
from jax import lax

D = 768
BLOCK = 256
SB_DEV = 8
KMAX = 24
NSB = 256
NS = 65536
NTB = 32
NT = 8192


def block_lists(key):
    key_heavy, key_light, key_large, key_pick, key_perm = jax.random.split(key, 5)
    groups = NSB // SB_DEV
    heavy = jax.random.randint(key_heavy, (groups,), 0, 4) == 0
    heavy_rows = jnp.repeat(heavy, SB_DEV)
    light = jax.random.randint(key_light, (NSB,), max(KMAX * 3 // 8, 1), KMAX * 3 // 4 + 1)
    large = jax.random.randint(key_large, (NSB,), KMAX * 3 // 4, KMAX + 1)
    tallies = jnp.where(heavy_rows, large, light)
    chosen = jax.random.randint(key_pick, (), 0, NSB)
    tallies = tallies.at[chosen].set(KMAX)
    keys = jax.random.split(key_perm, NSB)
    lists = jax.vmap(lambda single: jax.random.permutation(single, NTB)[:KMAX])(keys)
    return (lists.astype(jnp.int32), tallies.astype(jnp.int32))


def embed_values(key, count):
    key_base = jax.random.fold_in(key, 0)
    values = jnp.clip(jax.random.normal(key_base, (count, D), jnp.float32), -5.0, 5.0)
    return values.astype(jnp.bfloat16)


def draw_active_blocks(key, part):
    lists, tallies = block_lists(key)
    return lists


def draw_active_count(key, part):
    lists, tallies = block_lists(key)
    return tallies


def draw_source_embed(key, part):
    key = jax.random.fold_in(key, 11)
    return embed_values(key, NS)


def draw_target_embed(key, part):
    key = jax.random.fold_in(key, 23)
    return embed_values(key, NT)


def levels(key, extent, pieces, least, top_value):
    def one(dim, blocks):
        steps = jax.random.uniform(jax.random.fold_in(jax.random.fold_in(key, 6), dim), (blocks,), jnp.float32, least / len(pieces), top_value / len(pieces))
        return jnp.repeat(jnp.exp(steps), extent[dim] // blocks).reshape((-1,) + (1,) * (len(extent) - dim - 1))

    loudness = one(*pieces[0])
    for cut in pieces[1:]:
        loudness = loudness * one(*cut)
    return loudness


def setup_inputs(seed: int = 0) -> dict:
    key_list = jax.random.split(jax.random.key(seed), 7)
    return {
        "source_embed": draw_source_embed(jax.random.fold_in(key_list[6], 71), 0),
        "target_embed": draw_target_embed(jax.random.fold_in(key_list[6], 71), 0),
        "source_potential": jnp.clip(-7.0 + 3.0 * jax.random.uniform(key_list[2], (NS,), jnp.float32) ** levels(key_list[2], (NS,), ((0, 32),), -0.2, 0.2), -7.0, -4.0),
        "target_potential": jnp.clip(jax.random.uniform(key_list[3], (NT,), jnp.float32, -5.5, -3.5), -5.5, -3.5),
        "active_blocks": draw_active_blocks(jax.random.fold_in(key_list[6], 71), 0),
        "active_count": draw_active_count(jax.random.fold_in(key_list[6], 71), 0),
    }


def tile_plan(rows_block, pots_block, targ_block, tpot_block):
    scores = jnp.dot(rows_block, targ_block.T, preferred_element_type=jnp.float32)
    scale = 2.0 / math.sqrt(D)
    return jnp.exp(pots_block[:, None] + tpot_block[None, :] + scores * scale).astype(jnp.bfloat16)

def reference(source_embed, target_embed, source_potential, target_potential, active_blocks, active_count):
    rows_all = source_embed.reshape(NSB, BLOCK, D)
    pots_all = source_potential.reshape(NSB, BLOCK)

    def one_block(target_grads, inputs):
        rows_block, pots_block, id_list, tally = inputs

        def one_tile(entry, state):
            source_acc, target_acc = state
            start = (id_list[entry] * BLOCK).astype(jnp.int32)
            targ_block = lax.dynamic_slice_in_dim(target_embed, start, BLOCK, 0)
            tpot_block = lax.dynamic_slice_in_dim(target_potential, start, BLOCK, 0)
            plan = tile_plan(rows_block, pots_block, targ_block, tpot_block)
            source_acc = source_acc + jnp.dot(plan, targ_block, preferred_element_type=jnp.float32)
            current = lax.dynamic_slice_in_dim(target_acc, start, BLOCK, 0)
            added = current + jnp.dot(plan.T, rows_block, preferred_element_type=jnp.float32)
            target_acc = lax.dynamic_update_slice_in_dim(target_acc, added, start, 0)
            return (source_acc, target_acc)
        source_acc, target_grads = lax.fori_loop(0, tally, one_tile, (jnp.zeros((BLOCK, D), jnp.float32), target_grads))
        return (target_grads, source_acc)
    target_grads, source_grads = lax.scan(one_block, jnp.zeros((NT, D), jnp.float32), (rows_all, pots_all, active_blocks, active_count))
    return (source_grads.reshape(NS, D).astype(jnp.bfloat16), target_grads.astype(jnp.bfloat16))
```

```python
import functools
import math

import jax
import jax.numpy as jnp
from jax import lax
from jax.experimental import pallas as pl
from jax.experimental.pallas import tpu as pltpu
from jax.sharding import PartitionSpec as P

D = 768
BLOCK = 256
ROWS = 2048
LOG2E = 1.4426950408889634
SCALE = 2.0 / math.sqrt(D) * LOG2E
MESH = pl.DeviceIdType.MESH
F32 = jnp.float32
BF16 = jnp.bfloat16


def kernel(
    s_hbm, t_hbm, sp_ref, tp_ref, ids_ref, cnt_ref, gs_out, gt_out,
    s_v, t_v, plan, bias,
    z_part, z_send, z_recv, z_out,
    t_part, c_send, c_recv, x_send, x_recv, y_part, y_send, y_recv, g_out,
    load_sem, zs, zr, zo, cs, cr, xs, xr, ys, yr, ags, agr, ls, ks, kr,
):
    src = lax.axis_index("src")
    z = lax.axis_index("tgt")
    x = src // 8
    y = (src // 2) % 4
    core = src % 2

    def at(x_, y_, core_, z_):
        return ((x_ * 4 + y_) * 2 + core_, z_)

    def along(path, step):
        if path == 0:
            return at((x + step) % 4, y, core, z)
        return at(x, (y + step) % 4, core, z)

    def along_z(step):
        return at(x, y, core, (z + step) % 4)

    other = at(x, y, 1 - core, z)
    peers = [along_z(1), along_z(3), other]
    peers += [along(p, d) for p in (0, 1) for d in (1, 2, 3)]

    barrier = pltpu.get_barrier_semaphore()
    for peer in peers:
        pl.semaphore_signal(barrier, inc=1, device_id=peer, device_id_type=MESH)

    t_load = pltpu.make_async_copy(t_hbm, t_v, load_sem.at[0])
    s0_load = pltpu.make_async_copy(
        s_hbm.at[pl.ds(0, 512)], s_v.at[pl.ds(0, 512)], load_sem.at[1]
    )
    s1_load = pltpu.make_async_copy(
        s_hbm.at[pl.ds(512, 1536)], s_v.at[pl.ds(512, 1536)], load_sem.at[2]
    )
    t_load.start()
    s0_load.start()
    s1_load.start()

    sub = lax.broadcasted_iota(jnp.int32, (8, 24), 0)
    lane = lax.broadcasted_iota(jnp.int32, (8, 24), 1)
    count = jnp.zeros((8, 24), jnp.int32)
    for a in range(8):
        count = jnp.where(sub == a, cnt_ref[a], count)
    ids = jnp.where(lane < count, ids_ref[...], -1)
    tp = tp_ref[pl.ds(pl.multiple_of(z * 16, 16), 16), :] * LOG2E
    for b in range(8):
        hit = jnp.max(jnp.where(ids == z * 8 + b, 1.0, 0.0), axis=1, keepdims=True)
        for h in range(2):
            row = tp[2 * b + h:2 * b + h + 1, :]
            bias[:, b * 256 + h * 128:b * 256 + (h + 1) * 128] = jnp.where(
                hit > 0.5, row, -1e30
            )

    def remote(src_ref, dst_ref, send, recv, dev):
        return pltpu.make_async_remote_copy(
            src_ref=src_ref, dst_ref=dst_ref, send_sem=send, recv_sem=recv,
            device_id=dev, device_id_type=MESH,
        )

    def score(first, blocks):
        rows = blocks * BLOCK
        base = pl.multiple_of(first * BLOCK, BLOCK)
        lhs = s_v[pl.ds(base, rows), :]
        pots = []
        for h in range(2 * blocks):
            row = sp_ref[pl.ds(first * 2 + h, 1), :] * LOG2E
            pots.append(jnp.transpose(jnp.broadcast_to(row, (128, 128))))
        for n in range(4):
            cols = slice(n * 512, (n + 1) * 512)
            s = lax.dot_general(
                lhs, t_v[cols, :], (((1,), (1,)), ((), ())), preferred_element_type=F32
            )
            for i in range(blocks):
                tpr = bias[pl.ds(first + i, 1), cols]
                for h in range(2):
                    q = 2 * i + h
                    part = s[q * 128:(q + 1) * 128, :]
                    pot = jnp.concatenate([pots[q]] * 4, axis=1)
                    e = jnp.exp2(part * SCALE + (pot + tpr))
                    plan[pl.ds(base + q * 128, 128), cols] = e.astype(BF16)

    def z_copy(a, m):
        return remote(
            z_send.at[a, m], z_recv.at[a, m], zs.at[a, m], zr.at[a, m],
            along_z(1 if m % 2 == 0 else 3),
        )

    lane_low = lax.broadcasted_iota(jnp.int32, (128, 128), 1) < 64

    def source_block(a):
        base = pl.multiple_of(a * BLOCK, BLOCK)
        g = jnp.dot(plan[pl.ds(base, BLOCK), :], t_v[...], preferred_element_type=F32)
        for o, tile in ((0, 0), (1, 2), (2, 3), (3, 5)):
            z_part[a, o, 0:256, :] = g[:, tile * 128:(tile + 1) * 128]
        for o, tile in ((0, 1), (2, 4)):
            top = g[0:128, tile * 128:(tile + 1) * 128]
            low = g[128:256, tile * 128:(tile + 1) * 128]
            z_part[a, o, 256:384, :] = jnp.where(lane_low, top, pltpu.roll(low, 64, 1))
            z_part[a, o + 1, 256:384, :] = jnp.where(lane_low, pltpu.roll(top, 64, 1), low)
        for m, (o, r) in enumerate(((2, 0), (2, 192), (1, 192), (3, 0))):
            z_send[a, m] = z_part[a, (z + o) % 4, r:r + 192, :].astype(BF16)
            z_copy(a, m).start()

    def z_second(a):
        for m, o, r in ((0, 1, 0), (1, 3, 192)):
            z_copy(a, m).wait_recv()
            total = z_part[a, (z + o) % 4, r:r + 192, :] + z_recv[a, m].astype(F32)
            z_send[a, 4 + m] = total.astype(BF16)
            z_copy(a, 4 + m).start()

    def z_out_copy(a):
        rows = pl.ds(pl.multiple_of(a * BLOCK, BLOCK), BLOCK)
        return pltpu.make_async_copy(z_out.at[rows], gs_out.at[rows], zo.at[a])

    def z_final(a):
        for m in (2, 3, 4, 5):
            z_copy(a, m).wait_recv()
        first = z_part[a, z, 0:192, :] + (
            z_recv[a, 4].astype(F32) + z_recv[a, 3].astype(F32)
        )
        second = z_part[a, z, 192:384, :] + (
            z_recv[a, 2].astype(F32) + z_recv[a, 5].astype(F32)
        )
        whole = jnp.concatenate([first, second], axis=0)
        packed = whole[256:384, :]
        rolled = pltpu.roll(packed, 64, 1)
        odd = (z % 2) == 1
        for h in range(2):
            full = whole[h * 128:(h + 1) * 128, :]
            half = packed if h == 0 else rolled
            turned = pltpu.roll(full, 64, 1)
            left = jnp.where(odd, jnp.where(lane_low, half, turned), full)
            right = jnp.where(odd, turned, half)
            rows = pl.ds(pl.multiple_of(a * BLOCK + h * 128, 128), 128)
            z_out[rows, 0:128] = left.astype(BF16)
            z_out[rows, 128:192] = right[:, 0:64].astype(BF16)
        z_out_copy(a).start()

    def c_copy(c):
        return remote(c_send.at[c], c_recv.at[c], cs.at[c], cr.at[c], other)

    def target_chunk(c):
        cols = pl.ds(pl.multiple_of(c * 512, 512), 512)
        g = lax.dot_general(
            plan[:, cols], s_v[...], (((0,), (0,)), ((), ())), preferred_element_type=F32
        )
        t_part[c, 0] = g[0:256, :]
        t_part[c, 1] = g[256:512, :]
        c_send[c] = t_part[c, 1 - core].astype(BF16)
        c_copy(c).start()

    def x_copy(c, p, m):
        return remote(
            x_send.at[c, p, m], x_recv.at[c, p, m], xs.at[c, p, m], xr.at[c, p, m],
            along(p, 1 if m % 2 == 0 else 3),
        )

    def first_of(p):
        return x if p == 0 else y

    def second_of(p):
        return y if p == 0 else x

    def cols_of(p):
        return slice(p * 384, (p + 1) * 384)

    def rows_at(start, size):
        return pl.ds(pl.multiple_of(start, 16), size)

    def x_first(c):
        c_copy(c).wait_recv()
        t_part[c, core] = t_part[c, core] + c_recv[c].astype(F32)
        for m, (o, r) in enumerate(((2, 0), (2, 32), (1, 32), (3, 0))):
            for p in range(2):
                piece = (first_of(p) + o) % 4
                x_send[c, p, m] = t_part[
                    c, core, rows_at(piece * 64 + r, 32), cols_of(p)
                ].astype(BF16)
                x_copy(c, p, m).start()

    def x_second(c):
        for m, o, r in ((0, 1, 0), (1, 3, 32)):
            for p in range(2):
                piece = (first_of(p) + o) % 4
                x_copy(c, p, m).wait_recv()
                total = t_part[
                    c, core, rows_at(piece * 64 + r, 32), cols_of(p)
                ] + x_recv[c, p, m].astype(F32)
                x_send[c, p, 4 + m] = total.astype(BF16)
                x_copy(c, p, 4 + m).start()

    def y_copy(c, p, d):
        piece = (second_of(p) + d) % 4
        return remote(
            y_send.at[c, p, rows_at(piece * 16, 16)], y_recv.at[c, p, d - 1],
            ys.at[c, p, d - 1], yr.at[c, p, d - 1], along(1 - p, d),
        )

    def x_third(c):
        for p in range(2):
            for m in (2, 3, 4, 5):
                x_copy(c, p, m).wait_recv()
            mine = first_of(p) * 64
            low = t_part[c, core, rows_at(mine, 32), cols_of(p)] + (
                x_recv[c, p, 4].astype(F32) + x_recv[c, p, 3].astype(F32)
            )
            high = t_part[c, core, rows_at(mine + 32, 32), cols_of(p)] + (
                x_recv[c, p, 2].astype(F32) + x_recv[c, p, 5].astype(F32)
            )
            y_part[c, p, 0:32, :] = low
            y_part[c, p, 32:64, :] = high
            y_send[c, p, 0:32, :] = low.astype(BF16)
            y_send[c, p, 32:64, :] = high.astype(BF16)
            for d in (1, 2, 3):
                y_copy(c, p, d).start()

    def y_gather(c, p, d):
        rows = rows_at(first_of(p) * 64 + second_of(p) * 16, 16)
        piece = g_out.at[c, rows, cols_of(p)]
        return remote(piece, piece, ys.at[c, p, 2 + d], yr.at[c, p, 2 + d], along(1 - p, d))

    def y_final(c):
        for p in range(2):
            for d in (1, 2, 3):
                y_copy(c, p, d).wait_recv()
            mine = y_part[c, p, rows_at(second_of(p) * 16, 16), :]
            total = mine + (
                y_recv[c, p, 0].astype(F32)
                + y_recv[c, p, 1].astype(F32)
                + y_recv[c, p, 2].astype(F32)
            )
            rows = rows_at(first_of(p) * 64 + second_of(p) * 16, 16)
            g_out[c, rows, cols_of(p)] = total.astype(BF16)
            for d in (1, 2, 3):
                y_gather(c, p, d).start()

    def a_copy(c, p, m):
        start = first_of(p) * 64
        size = 64
        if m == 2:
            start, size = ((first_of(p) + 3) % 4) * 64, 32
        if m == 3:
            start, size = ((first_of(p) + 1) % 4) * 64 + 32, 32
        piece = g_out.at[c, rows_at(start, size), cols_of(p)]
        return remote(
            piece, piece, ags.at[c, p, m], agr.at[c, p, m], along(p, 1 if m % 2 == 0 else 3)
        )

    def gather_first(c):
        for p in range(2):
            for d in (1, 2, 3):
                y_gather(c, p, d).wait_recv()
            for m in (0, 1):
                a_copy(c, p, m).start()

    def gather_second(c):
        for m in (0, 1):
            for p in range(2):
                a_copy(c, p, m).wait_recv()
                a_copy(c, p, 2 + m).start()

    def out_rows(c):
        return pl.ds(pl.multiple_of(c * 512 + core * 256, 256), 256)

    def l_copy(c):
        return pltpu.make_async_copy(g_out.at[c], gt_out.at[out_rows(c)], ls.at[c])

    def k_copy(c):
        return remote(g_out.at[c], gt_out.at[out_rows(c)], ks.at[c], kr.at[c], other)

    def gather_final(c):
        for m in (2, 3):
            for p in range(2):
                a_copy(c, p, m).wait_recv()
        k_copy(c).start()
        l_copy(c).start()

    t_load.wait()
    s0_load.wait()
    score(0, 1)
    pl.semaphore_wait(barrier, len(peers))

    @pl.loop(0, 2)
    def _(a):
        source_block(a)

        @pl.when(a == 0)
        def _():
            score(1, 1)

    s1_load.wait()

    @pl.loop(1, 4)
    def _(d):
        score(d * 2, 2)

        @pl.when(d >= 2)
        def _():
            z_second(d - 2)

    def when(cond, fn, arg):
        @pl.when(cond)
        def _():
            fn(arg)

    @pl.loop(0, 11)
    def _(i):
        when(i < 6, source_block, i + 2)
        when((i >= 1) & (i < 5), x_first, i - 1)
        when(i < 4, target_chunk, i)
        when((i >= 1) & (i < 5), x_second, i - 1)
        when((i >= 2) & (i < 6), x_third, i - 2)
        when((i >= 3) & (i < 7), y_final, i - 3)
        when((i >= 4) & (i < 8), gather_first, i - 4)
        when((i >= 5) & (i < 9), gather_second, i - 5)
        when((i >= 6) & (i < 10), gather_final, i - 6)
        second = jnp.where(i < 5, i + 1, i - 2)
        when(((i >= 1) & (i < 5)) | ((i >= 8) & (i < 10)), z_second, second)
        when((i >= 1) & (i < 7), z_final, i - 1)

    z_final(6)
    z_final(7)

    @pl.loop(0, 4)
    def _(c):
        k_copy(c).wait()
        l_copy(c).wait()
        c_copy(c).wait_send()
        for p in range(2):
            for m in range(6):
                x_copy(c, p, m).wait_send()
            for d in (1, 2, 3):
                y_copy(c, p, d).wait_send()
                y_gather(c, p, d).wait_send()
            for m in range(4):
                a_copy(c, p, m).wait_send()

    @pl.loop(0, 8)
    def _(a):
        for m in range(6):
            z_copy(a, m).wait_send()
        z_out_copy(a).wait()


def shards(
    source_embed, target_embed, source_potential, target_potential, active_blocks, active_count
):
    vmem = pl.BlockSpec(memory_space=pltpu.VMEM)
    smem = pl.BlockSpec(memory_space=pltpu.SMEM)
    hbm = pl.BlockSpec(memory_space=pl.ANY)
    dma = pltpu.SemaphoreType.DMA
    return pl.pallas_call(
        kernel,
        out_shape=(
            jax.ShapeDtypeStruct((ROWS, D // 4), BF16),
            jax.ShapeDtypeStruct((ROWS, D), BF16),
        ),
        in_specs=[hbm, hbm, vmem, vmem, vmem, smem],
        out_specs=(hbm, hbm),
        scratch_shapes=[
            pltpu.VMEM((ROWS, D), BF16),
            pltpu.VMEM((ROWS, D), BF16),
            pltpu.VMEM((ROWS, ROWS), BF16),
            pltpu.VMEM((8, ROWS), F32),
            pltpu.VMEM((8, 4, 384, 128), F32),
            pltpu.VMEM((8, 6, 192, 128), BF16),
            pltpu.VMEM((8, 6, 192, 128), BF16),
            pltpu.VMEM((ROWS, D // 4), BF16),
            pltpu.VMEM((4, 2, 256, D), F32),
            pltpu.VMEM((4, 256, D), BF16),
            pltpu.VMEM((4, 256, D), BF16),
            pltpu.VMEM((4, 2, 6, 32, 384), BF16),
            pltpu.VMEM((4, 2, 6, 32, 384), BF16),
            pltpu.VMEM((4, 2, 64, 384), F32),
            pltpu.VMEM((4, 2, 64, 384), BF16),
            pltpu.VMEM((4, 2, 3, 16, 384), BF16),
            pltpu.VMEM((4, 256, D), BF16),
            dma((3,)),
            dma((8, 6)),
            dma((8, 6)),
            dma((8,)),
            dma((4,)),
            dma((4,)),
            dma((4, 2, 6)),
            dma((4, 2, 6)),
            dma((4, 2, 6)),
            dma((4, 2, 6)),
            dma((4, 2, 4)),
            dma((4, 2, 4)),
            dma((4,)),
            dma((4,)),
            dma((4,)),
        ],
        compiler_params=pltpu.CompilerParams(
            collective_id=0, has_side_effects=True, vmem_limit_bytes=56 * 2**20
        ),
        cost_estimate=pl.CostEstimate(
            flops=3 * 2 * ROWS * ROWS * D, bytes_accessed=12 * 2**20, transcendentals=ROWS * ROWS
        ),
    )(
        source_embed,
        target_embed,
        source_potential.reshape(16, 128),
        target_potential.reshape(64, 128),
        active_blocks,
        active_count,
    )


def solution(mesh):
    return jax.shard_map(
        shards,
        mesh=mesh,
        in_specs=(P("src", None), P("tgt", None), P("src"), P(), P("src", None), P("src")),
        out_specs=(P("src", "tgt"), P("tgt", None)),
        check_vma=False,
    )
```

```python
import functools
import math

import jax
import jax.numpy as jnp
from jax import lax
from jax.experimental import pallas as pl
from jax.experimental.pallas import tpu as pltpu
from jax.sharding import PartitionSpec as P

D = 768
BLOCK = 256
ROWS = 2048
LOG2E = 1.4426950408889634
SCALE = 2.0 / math.sqrt(D) * LOG2E
MESH = pl.DeviceIdType.MESH
F32 = jnp.float32
BF16 = jnp.bfloat16

SCHEDULE = (
    ("S00", "S01", "S02", "S03", "G0",),
    ("G1",),
    ("S10",),
    ("S11",),
    ("S12",),
    ("S13",),
    ("S20", "S30",),
    ("T0",),
    ("S21", "S31",),
    ("B0",),
    ("X0",),
    ("T1",),
    ("B1",),
    ("G2",),
    ("X1",),
    ("S22", "S32",),
    ("T2",),
    ("Y0",),
    ("G3",),
    ("X2",),
    ("S23", "S33",),
    ("T3",),
    ("Y1",),
    ("F0",),
    ("B2",),
    ("G4",),
    ("X3",),
    ("B3",),
    ("G5",),
    ("Y2",),
    ("F1",),
    ("H0",),
    ("G6",),
    ("G7",),
    ("B4",),
    ("F2",),
    ("Y3",),
    ("H1",),
    ("I0",),
    ("B5",),
    ("C0",),
    ("F3",),
    ("H2",),
    ("B6",),
    ("C1",),
    ("B7",),
    ("C2",),
    ("I1",),
    ("C3",),
    ("H3",),
    ("I2",),
    ("C4",),
    ("C5",),
    ("C6",),
    ("I3",),
    ("C7",),
)


def kernel(
    s_hbm, t_hbm, sp_ref, tp_ref, ids_ref, cnt_ref, gs_out, gt_out,
    s_v, t_v, plan, bias,
    z_part, z_send, z_recv, z2_send, z2_recv, z_out,
    t_part, c_send, c_recv, x_send, x_recv, y_part, y_send, y_recv, g_out,
    load_sem, zs, zr, zo, cs, cr, xs, xr, ys, yr, ags, agr, ls, ks, kr,
):
    src = lax.axis_index("src")
    z = lax.axis_index("tgt")
    x = src // 8
    y = (src // 2) % 4
    core = src % 2

    def at(x_, y_, core_, z_):
        return ((x_ * 4 + y_) * 2 + core_, z_)

    def along(path, step):
        if path == 0:
            return at((x + step) % 4, y, core, z)
        return at(x, (y + step) % 4, core, z)

    def along_z(step):
        return at(x, y, core, (z + step) % 4)

    other = at(x, y, 1 - core, z)
    peers = [along_z(1), along_z(3), other]
    peers += [along(p, d) for p in (0, 1) for d in (1, 2, 3)]

    barrier = pltpu.get_barrier_semaphore()
    for peer in peers:
        pl.semaphore_signal(barrier, inc=1, device_id=peer, device_id_type=MESH)

    def load(n, hbm_ref, ref, start, size):
        rows = pl.ds(start, size)
        return pltpu.make_async_copy(hbm_ref.at[rows], ref.at[rows], load_sem.at[n])

    loads = [load(0, s_hbm, s_v, 0, 512)]
    loads += [load(1 + n, t_hbm, t_v, n * 512, 512) for n in range(4)]
    loads += [load(5, s_hbm, s_v, 512, 1536)]
    for copy in loads:
        copy.start()

    sub = lax.broadcasted_iota(jnp.int32, (8, 24), 0)
    lane = lax.broadcasted_iota(jnp.int32, (8, 24), 1)
    count = jnp.zeros((8, 24), jnp.int32)
    for a in range(8):
        count = jnp.where(sub == a, cnt_ref[a], count)
    ids = jnp.where(lane < count, ids_ref[...], -1)
    tp = tp_ref[pl.ds(pl.multiple_of(z * 16, 16), 16), :] * LOG2E
    for b in range(8):
        hit = jnp.max(jnp.where(ids == z * 8 + b, 1.0, 0.0), axis=1, keepdims=True)
        for h in range(2):
            row = tp[2 * b + h:2 * b + h + 1, :]
            bias[:, b * 256 + h * 128:b * 256 + (h + 1) * 128] = jnp.where(
                hit > 0.5, row, -1e30
            )

    def remote(src_ref, dst_ref, send, recv, dev):
        return pltpu.make_async_remote_copy(
            src_ref=src_ref, dst_ref=dst_ref, send_sem=send, recv_sem=recv,
            device_id=dev, device_id_type=MESH,
        )

    def score(first, blocks, n):
        rows = blocks * BLOCK
        base = first * BLOCK
        cols = slice(n * 512, (n + 1) * 512)
        s = lax.dot_general(
            s_v[base:base + rows, :], t_v[cols, :], (((1,), (1,)), ((), ())),
            preferred_element_type=F32,
        )
        for i in range(blocks):
            tpr = bias[first + i:first + i + 1, cols]
            for h in range(2):
                q = 2 * i + h
                row = sp_ref[first * 2 + q:first * 2 + q + 1, :] * LOG2E
                pot = jnp.transpose(jnp.broadcast_to(row, (128, 128)))
                pot = jnp.concatenate([pot] * 4, axis=1)
                e = jnp.exp2(s[q * 128:(q + 1) * 128, :] * SCALE + (pot + tpr))
                plan[base + q * 128:base + (q + 1) * 128, cols] = e.astype(BF16)

    def z_copy(a, m):
        first, way = m < 2, m % 2
        return remote(
            z_send.at[a, way] if first else z2_send.at[a, way],
            z_recv.at[a, way] if first else z2_recv.at[a, way],
            zs.at[a, m], zr.at[a, m], along_z(1 if way == 0 else 3),
        )

    lane_low = lax.broadcasted_iota(jnp.int32, (128, 128), 1) < 64

    def source_body(first, blocks):
        base = first * BLOCK
        whole = jnp.dot(
            plan[base:base + blocks * BLOCK, :], t_v[...], preferred_element_type=F32
        )
        for i in range(blocks):
            a = first + i
            g = whole[i * BLOCK:(i + 1) * BLOCK, :]
            for o, tile in ((0, 0), (1, 2), (2, 3), (3, 5)):
                z_part[a, o, 0:256, :] = g[:, tile * 128:(tile + 1) * 128]
            for o, tile in ((0, 1), (2, 4)):
                top = g[0:128, tile * 128:(tile + 1) * 128]
                low = g[128:256, tile * 128:(tile + 1) * 128]
                z_part[a, o, 256:384, :] = jnp.where(lane_low, top, pltpu.roll(low, 64, 1))
                z_part[a, o + 1, 256:384, :] = jnp.where(lane_low, pltpu.roll(top, 64, 1), low)
            for way, half, o, r in ((0, 0, 2, 0), (0, 1, 1, 192), (1, 0, 2, 192), (1, 1, 3, 0)):
                z_send[a, way, half * 192:half * 192 + 192, :] = z_part[
                    a, (z + o) % 4, r:r + 192, :
                ].astype(BF16)

    def pair_start(pair):
        source_start(2 * pair)
        source_start(2 * pair + 1)

    def source_start(a):
        for m in (0, 1):
            z_copy(a, m).start()

    def second_wait(a):
        for m in (0, 1):
            z_copy(a, m).wait_recv()

    def second_body(a):
        for way, o, r in ((0, 1, 0), (1, 3, 192)):
            total = z_part[a, (z + o) % 4, r:r + 192, :] + z_recv[a, way, 0:192, :].astype(F32)
            z2_send[a, way] = total.astype(BF16)

    def second_start(a):
        for m in (2, 3):
            z_copy(a, m).start()

    def z_out_copy(a):
        cols = pl.ds(pl.multiple_of(a * BLOCK, BLOCK), BLOCK)
        return pltpu.make_async_copy(z_out.at[:, cols], gs_out.at[:, cols], zo.at[a])

    def final_wait(a):
        for m in (2, 3):
            z_copy(a, m).wait_recv()

    def final_body(a):
        first = z_part[a, z, 0:192, :] + (
            z2_recv[a, 0].astype(F32) + z_recv[a, 1, 192:384, :].astype(F32)
        )
        second = z_part[a, z, 192:384, :] + (
            z_recv[a, 0, 192:384, :].astype(F32) + z2_recv[a, 1].astype(F32)
        )
        whole = jnp.concatenate([first, second], axis=0)
        packed = whole[256:384, :]
        rolled = pltpu.roll(packed, 64, 1)
        odd = (z % 2) == 1
        for h in range(2):
            full = whole[h * 128:(h + 1) * 128, :]
            half = packed if h == 0 else rolled
            turned = pltpu.roll(full, 64, 1)
            left = jnp.where(odd, jnp.where(lane_low, half, turned), full)
            right = jnp.where(odd, turned, half)
            cols = pl.ds(pl.multiple_of(a * BLOCK + h * 128, 128), 128)
            z_out[0:128, cols] = jnp.transpose(left).astype(BF16)
            z_out[128:192, cols] = jnp.transpose(right)[0:64, :].astype(BF16)

    def final_start(a):
        z_out_copy(a).start()
        for m in range(4):
            z_copy(a, m).wait_send()

    def c_copy(c):
        return remote(c_send.at[c], c_recv.at[c], cs.at[c], cr.at[c], other)

    def target_body(c):
        cols = slice(c * 512, (c + 1) * 512)
        g = lax.dot_general(
            plan[:, cols], s_v[...], (((0,), (0,)), ((), ())), preferred_element_type=F32
        )
        low, high = g[0:256, :], g[256:512, :]
        t_part[c] = jnp.where(core == 0, low, high)
        c_send[c] = jnp.where(core == 0, high, low).astype(BF16)

    def target_start(c):
        c_copy(c).start()

    def x_copy(c, p, d):
        return remote(
            x_send.at[c, p, d - 1], x_recv.at[c, p, d - 1],
            xs.at[c, p, d - 1], xr.at[c, p, d - 1], along(p, d),
        )

    def first_of(p):
        return x if p == 0 else y

    def second_of(p):
        return y if p == 0 else x

    def cols_of(p):
        return slice(p * 384, (p + 1) * 384)

    def rows_at(start, size):
        return pl.ds(pl.multiple_of(start, 16), size)

    def x_wait(c):
        c_copy(c).wait_recv()

    def x_body(c):
        t_part[c] = t_part[c] + c_recv[c].astype(F32)
        for d in (1, 2, 3):
            for p in range(2):
                piece = (first_of(p) + d) % 4
                x_send[c, p, d - 1] = t_part[
                    c, rows_at(piece * 64, 64), cols_of(p)
                ].astype(BF16)

    def x_start(c):
        for d in (2, 1, 3):
            for p in range(2):
                x_copy(c, p, d).start()

    def y_copy(c, p, d):
        piece = (second_of(p) + d) % 4
        return remote(
            y_send.at[c, p, rows_at(piece * 16, 16)], y_recv.at[c, p, d - 1],
            ys.at[c, p, d - 1], yr.at[c, p, d - 1], along(1 - p, d),
        )

    def y_wait(c):
        for p in range(2):
            for d in (1, 3, 2):
                x_copy(c, p, d).wait_recv()

    def y_body(c):
        for p in range(2):
            total = t_part[c, rows_at(first_of(p) * 64, 64), cols_of(p)] + (
                x_recv[c, p, 0].astype(F32)
                + x_recv[c, p, 1].astype(F32)
                + x_recv[c, p, 2].astype(F32)
            )
            y_part[c, p] = total
            y_send[c, p] = total.astype(BF16)

    def y_start(c):
        for d in (2, 1, 3):
            for p in range(2):
                y_copy(c, p, d).start()
        c_copy(c).wait_send()
        for p in range(2):
            for d in (1, 2, 3):
                x_copy(c, p, d).wait_send()

    def y_gather(c, p, d):
        rows = rows_at(first_of(p) * 64 + second_of(p) * 16, 16)
        piece = g_out.at[c, rows, cols_of(p)]
        return remote(piece, piece, ys.at[c, p, 2 + d], yr.at[c, p, 2 + d], along(1 - p, d))

    def f_wait(c):
        for p in range(2):
            for d in (1, 2, 3):
                y_copy(c, p, d).wait_recv()

    def f_body(c):
        for p in range(2):
            mine = y_part[c, p, rows_at(second_of(p) * 16, 16), :]
            total = mine + (
                y_recv[c, p, 0].astype(F32)
                + y_recv[c, p, 1].astype(F32)
                + y_recv[c, p, 2].astype(F32)
            )
            rows = rows_at(first_of(p) * 64 + second_of(p) * 16, 16)
            g_out[c, rows, cols_of(p)] = total.astype(BF16)

    def f_start(c):
        for d in (2, 1, 3):
            for p in range(2):
                y_gather(c, p, d).start()
        for p in range(2):
            for d in (1, 2, 3):
                y_copy(c, p, d).wait_send()

    def a_copy(c, p, d):
        piece = g_out.at[c, rows_at(first_of(p) * 64, 64), cols_of(p)]
        return remote(
            piece, piece, ags.at[c, p, d - 1], agr.at[c, p, d - 1], along(p, d)
        )

    def out_rows(c):
        return pl.ds(pl.multiple_of(c * 512 + core * 256, 256), 256)

    def k_copy(c):
        return remote(g_out.at[c], gt_out.at[out_rows(c)], ks.at[c], kr.at[c], other)

    def l_copy(c):
        return pltpu.make_async_copy(g_out.at[c], gt_out.at[out_rows(c)], ls.at[c])

    def h_wait(c):
        for p in range(2):
            for d in (1, 2, 3):
                y_gather(c, p, d).wait_recv()

    def h_start(c):
        for d in (2, 1, 3):
            for p in range(2):
                a_copy(c, p, d).start()
        for p in range(2):
            for d in (1, 2, 3):
                y_gather(c, p, d).wait_send()

    def i_start(c):
        for p in range(2):
            for d in (1, 3, 2):
                a_copy(c, p, d).wait_recv()
        k_copy(c).start()
        l_copy(c).start()
        for p in range(2):
            for d in (1, 2, 3):
                a_copy(c, p, d).wait_send()

    def close(c):
        k_copy(c).wait()
        l_copy(c).wait()

    def nothing(_):
        pass

    ops = {
        "S": (nothing, None, nothing),
        "G": (nothing, lambda a: source_body(a, 1), source_start),
        "P": (nothing, lambda pair: source_body(2 * pair, 2), pair_start),
        "B": (second_wait, second_body, second_start),
        "C": (final_wait, final_body, final_start),
        "T": (nothing, target_body, target_start),
        "X": (x_wait, x_body, x_start),
        "Y": (y_wait, y_body, y_start),
        "F": (f_wait, f_body, f_start),
        "H": (h_wait, nothing, h_start),
        "I": (nothing, nothing, i_start),
    }
    for copy in loads[:5]:
        copy.wait()
    for index, block in enumerate(SCHEDULE):
        if index == 2:
            loads[5].wait()
        for op in block:
            ops[op[0]][0](int(op[1]))
        for op in block:
            if op[0] == "S":
                score(int(op[1]) * 2, 2, int(op[2]))
            else:
                ops[op[0]][1](int(op[1]))
        if index == 0:
            pl.semaphore_wait(barrier, len(peers))
        for op in block:
            ops[op[0]][2](int(op[1]))

    for c in range(4):
        close(c)
    for a in range(8):
        z_out_copy(a).wait()


def shards(
    source_embed, target_embed, source_potential, target_potential, active_blocks, active_count
):
    vmem = pl.BlockSpec(memory_space=pltpu.VMEM)
    smem = pl.BlockSpec(memory_space=pltpu.SMEM)
    hbm = pl.BlockSpec(memory_space=pl.ANY)
    dma = pltpu.SemaphoreType.DMA
    source_t, target = pl.pallas_call(
        kernel,
        out_shape=(
            jax.ShapeDtypeStruct((D // 4, ROWS), BF16),
            jax.ShapeDtypeStruct((ROWS, D), BF16),
        ),
        in_specs=[hbm, hbm, vmem, vmem, vmem, smem],
        out_specs=(hbm, hbm),
        scratch_shapes=[
            pltpu.VMEM((ROWS, D), BF16),
            pltpu.VMEM((ROWS, D), BF16),
            pltpu.VMEM((ROWS, ROWS), BF16),
            pltpu.VMEM((8, ROWS), F32),
            pltpu.VMEM((8, 4, 384, 128), F32),
            pltpu.VMEM((8, 2, 384, 128), BF16),
            pltpu.VMEM((8, 2, 384, 128), BF16),
            pltpu.VMEM((8, 2, 192, 128), BF16),
            pltpu.VMEM((8, 2, 192, 128), BF16),
            pltpu.VMEM((D // 4, ROWS), BF16),
            pltpu.VMEM((4, 256, D), F32),
            pltpu.VMEM((4, 256, D), BF16),
            pltpu.VMEM((4, 256, D), BF16),
            pltpu.VMEM((4, 2, 3, 64, 384), BF16),
            pltpu.VMEM((4, 2, 3, 64, 384), BF16),
            pltpu.VMEM((4, 2, 64, 384), F32),
            pltpu.VMEM((4, 2, 64, 384), BF16),
            pltpu.VMEM((4, 2, 3, 16, 384), BF16),
            pltpu.VMEM((4, 256, D), BF16),
            dma((6,)),
            dma((8, 4)),
            dma((8, 4)),
            dma((8,)),
            dma((4,)),
            dma((4,)),
            dma((4, 2, 3)),
            dma((4, 2, 3)),
            dma((4, 2, 6)),
            dma((4, 2, 6)),
            dma((4, 2, 3)),
            dma((4, 2, 3)),
            dma((4,)),
            dma((4,)),
            dma((4,)),
        ],
        compiler_params=pltpu.CompilerParams(
            collective_id=0, has_side_effects=True, vmem_limit_bytes=56 * 2**20
        ),
        cost_estimate=pl.CostEstimate(
            flops=3 * 2 * ROWS * ROWS * D, bytes_accessed=12 * 2**20, transcendentals=ROWS * ROWS
        ),
    )(
        source_embed,
        target_embed,
        source_potential.reshape(16, 128),
        target_potential.reshape(64, 128),
        active_blocks,
        active_count,
    )
    return source_t.T, target


def solution(mesh):
    return jax.shard_map(
        shards,
        mesh=mesh,
        in_specs=(P("src", None), P("tgt", None), P("src"), P(), P("src", None), P("src")),
        out_specs=(P("src", "tgt"), P("tgt", None)),
        check_vma=False,
    )
```

```python
import functools
import math

import jax
import jax.numpy as jnp
from jax import lax
from jax.experimental import pallas as pl
from jax.experimental.pallas import tpu as pltpu
from jax.sharding import PartitionSpec as P

D = 768
BLOCK = 256
ROWS = 2048
LOG2E = 1.4426950408889634
SCALE = 2.0 / math.sqrt(D) * LOG2E
MESH = pl.DeviceIdType.MESH
F32 = jnp.float32
BF16 = jnp.bfloat16

SCHEDULE = (
    ("S00", "S01", "S02", "S03", "G0",),
    ("G1",),
    ("S10",),
    ("S11",),
    ("S12",),
    ("S13",),
    ("S20", "S30",),
    ("T0",),
    ("S21", "S31",),
    ("B0",),
    ("X0",),
    ("T1",),
    ("B1",),
    ("G2",),
    ("X1",),
    ("S22", "S32",),
    ("T2",),
    ("Y0",),
    ("G3",),
    ("X2",),
    ("S23", "S33",),
    ("T3",),
    ("Y1",),
    ("F0",),
    ("B2",),
    ("G4",),
    ("X3",),
    ("B3",),
    ("G5",),
    ("Y2",),
    ("F1",),
    ("H0",),
    ("G6",),
    ("G7",),
    ("B4",),
    ("F2",),
    ("Y3",),
    ("H1",),
    ("I0",),
    ("B5",),
    ("C0",),
    ("F3",),
    ("H2",),
    ("B6",),
    ("C1",),
    ("B7",),
    ("C2",),
    ("I1",),
    ("C3",),
    ("H3",),
    ("I2",),
    ("C4",),
    ("C5",),
    ("C6",),
    ("I3",),
    ("C7",),
)


def kernel(
    s_hbm, t_hbm, sp_ref, tp_ref, ids_ref, cnt_ref, gs_out, gt_out,
    s_v, t_v, plan, bias,
    z_part, z_send, z_recv, z2_send, z2_recv, z_out,
    t_part, c_send, c_recv, x_send, x_recv, y_part, y_send, y_recv, g_out,
    load_sem, zs, zr, zo, cs, cr, xs, xr, ys, yr, ags, agr, ls, ks, kr,
):
    src = lax.axis_index("src")
    z = lax.axis_index("tgt")
    x = src // 8
    y = (src // 2) % 4
    core = src % 2

    def at(x_, y_, core_, z_):
        return ((x_ * 4 + y_) * 2 + core_, z_)

    def along(path, step):
        if path == 0:
            return at((x + step) % 4, y, core, z)
        return at(x, (y + step) % 4, core, z)

    def along_z(step):
        return at(x, y, core, (z + step) % 4)

    other = at(x, y, 1 - core, z)
    peers = [along_z(1), along_z(3), other]
    peers += [along(p, d) for p in (0, 1) for d in (1, 2, 3)]

    barrier = pltpu.get_barrier_semaphore()
    for peer in peers:
        pl.semaphore_signal(barrier, inc=1, device_id=peer, device_id_type=MESH)

    def load(n, hbm_ref, ref, start, size):
        rows = pl.ds(start, size)
        return pltpu.make_async_copy(hbm_ref.at[rows], ref.at[rows], load_sem.at[n])

    loads = [load(0, s_hbm, s_v, 0, 512)]
    loads += [load(1 + n, t_hbm, t_v, n * 512, 512) for n in range(4)]
    loads += [load(5, s_hbm, s_v, 512, 1536)]
    for copy in loads:
        copy.start()

    sub = lax.broadcasted_iota(jnp.int32, (8, 24), 0)
    lane = lax.broadcasted_iota(jnp.int32, (8, 24), 1)
    count = jnp.zeros((8, 24), jnp.int32)
    for a in range(8):
        count = jnp.where(sub == a, cnt_ref[a], count)
    ids = jnp.where(lane < count, ids_ref[...], -1)
    tp = tp_ref[pl.ds(pl.multiple_of(z * 16, 16), 16), :] * LOG2E
    for b in range(8):
        hit = jnp.max(jnp.where(ids == z * 8 + b, 1.0, 0.0), axis=1, keepdims=True)
        for h in range(2):
            row = tp[2 * b + h:2 * b + h + 1, :]
            bias[:, b * 256 + h * 128:b * 256 + (h + 1) * 128] = jnp.where(
                hit > 0.5, row, -1e30
            )

    def remote(src_ref, dst_ref, send, recv, dev):
        return pltpu.make_async_remote_copy(
            src_ref=src_ref, dst_ref=dst_ref, send_sem=send, recv_sem=recv,
            device_id=dev, device_id_type=MESH,
        )

    def score(first, blocks, n):
        rows = blocks * BLOCK
        base = first * BLOCK
        cols = slice(n * 512, (n + 1) * 512)
        s = lax.dot_general(
            s_v[base:base + rows, :], t_v[cols, :], (((1,), (1,)), ((), ())),
            preferred_element_type=F32,
        )
        for i in range(blocks):
            tpr = bias[first + i:first + i + 1, cols]
            for h in range(2):
                q = 2 * i + h
                row = sp_ref[first * 2 + q:first * 2 + q + 1, :] * LOG2E
                pot = jnp.transpose(jnp.broadcast_to(row, (128, 128)))
                pot = jnp.concatenate([pot] * 4, axis=1)
                e = jnp.exp2(s[q * 128:(q + 1) * 128, :] * SCALE + (pot + tpr))
                plan[base + q * 128:base + (q + 1) * 128, cols] = e.astype(BF16)

    def z_copy(a, m):
        first, way = m < 2, m % 2
        return remote(
            z_send.at[a, way] if first else z2_send.at[a, way],
            z_recv.at[a, way] if first else z2_recv.at[a, way],
            zs.at[a, m], zr.at[a, m], along_z(1 if way == 0 else 3),
        )

    lane_low = lax.broadcasted_iota(jnp.int32, (128, 128), 1) < 64

    def source_body(first, blocks):
        base = first * BLOCK
        whole = jnp.dot(
            plan[base:base + blocks * BLOCK, :], t_v[...], preferred_element_type=F32
        )
        for i in range(blocks):
            a = first + i
            g = whole[i * BLOCK:(i + 1) * BLOCK, :]
            for o, tile in ((0, 0), (1, 2), (2, 3), (3, 5)):
                z_part[a, o, 0:256, :] = g[:, tile * 128:(tile + 1) * 128]
            for o, tile in ((0, 1), (2, 4)):
                top = g[0:128, tile * 128:(tile + 1) * 128]
                low = g[128:256, tile * 128:(tile + 1) * 128]
                z_part[a, o, 256:384, :] = jnp.where(lane_low, top, pltpu.roll(low, 64, 1))
                z_part[a, o + 1, 256:384, :] = jnp.where(lane_low, pltpu.roll(top, 64, 1), low)
            for way, half, o, r in ((0, 0, 2, 0), (0, 1, 1, 192), (1, 0, 2, 192), (1, 1, 3, 0)):
                z_send[a, way, half * 192:half * 192 + 192, :] = z_part[
                    a, (z + o) % 4, r:r + 192, :
                ].astype(BF16)

    def pair_start(pair):
        source_start(2 * pair)
        source_start(2 * pair + 1)

    def source_start(a):
        for m in (0, 1):
            z_copy(a, m).start()

    def second_wait(a):
        for m in (0, 1):
            z_copy(a, m).wait_recv()

    def second_body(a):
        for way, o, r in ((0, 1, 0), (1, 3, 192)):
            total = z_part[a, (z + o) % 4, r:r + 192, :] + z_recv[a, way, 0:192, :].astype(F32)
            z2_send[a, way] = total.astype(BF16)

    def second_start(a):
        for m in (2, 3):
            z_copy(a, m).start()

    def z_out_copy(a):
        cols = pl.ds(pl.multiple_of(a * BLOCK, BLOCK), BLOCK)
        return pltpu.make_async_copy(z_out.at[:, cols], gs_out.at[:, cols], zo.at[a])

    def final_wait(a):
        for m in (2, 3):
            z_copy(a, m).wait_recv()

    def final_body(a):
        first = z_part[a, z, 0:192, :] + (
            z2_recv[a, 0].astype(F32) + z_recv[a, 1, 192:384, :].astype(F32)
        )
        second = z_part[a, z, 192:384, :] + (
            z_recv[a, 0, 192:384, :].astype(F32) + z2_recv[a, 1].astype(F32)
        )
        whole = jnp.concatenate([first, second], axis=0)
        packed = whole[256:384, :]
        rolled = pltpu.roll(packed, 64, 1)
        odd = (z % 2) == 1
        for h in range(2):
            full = whole[h * 128:(h + 1) * 128, :]
            half = packed if h == 0 else rolled
            turned = pltpu.roll(full, 64, 1)
            left = jnp.where(odd, jnp.where(lane_low, half, turned), full)
            right = jnp.where(odd, turned, half)
            cols = pl.ds(pl.multiple_of(a * BLOCK + h * 128, 128), 128)
            z_out[0:128, cols] = jnp.transpose(left).astype(BF16)
            z_out[128:192, cols] = jnp.transpose(right)[0:64, :].astype(BF16)

    def final_start(a):
        z_out_copy(a).start()
        for m in range(4):
            z_copy(a, m).wait_send()

    def c_copy(c):
        return remote(c_send.at[c], c_recv.at[c], cs.at[c], cr.at[c], other)

    def target_body(c):
        cols = slice(c * 512, (c + 1) * 512)
        g = lax.dot_general(
            plan[:, cols], s_v[...], (((0,), (0,)), ((), ())), preferred_element_type=F32
        )
        low, high = g[0:256, :], g[256:512, :]
        t_part[c] = jnp.where(core == 0, low, high)
        c_send[c] = jnp.where(core == 0, high, low).astype(BF16)

    def target_start(c):
        c_copy(c).start()

    def x_copy(c, p, d):
        return remote(
            x_send.at[c, p, d - 1], x_recv.at[c, p, d - 1],
            xs.at[c, p, d - 1], xr.at[c, p, d - 1], along(p, d),
        )

    def first_of(p):
        return x if p == 0 else y

    def second_of(p):
        return y if p == 0 else x

    def cols_of(p):
        return slice(p * 384, (p + 1) * 384)

    def rows_at(start, size):
        return pl.ds(pl.multiple_of(start, 16), size)

    def x_wait(c):
        c_copy(c).wait_recv()

    def x_body(c):
        t_part[c] = t_part[c] + c_recv[c].astype(F32)
        for d in (1, 2, 3):
            for p in range(2):
                piece = (first_of(p) + d) % 4
                x_send[c, p, d - 1] = t_part[
                    c, rows_at(piece * 64, 64), cols_of(p)
                ].astype(BF16)

    def x_start(c):
        for d in (2, 1, 3):
            for p in range(2):
                x_copy(c, p, d).start()

    def y_copy(c, p, d):
        piece = (second_of(p) + d) % 4
        return remote(
            y_send.at[c, p, rows_at(piece * 16, 16)], y_recv.at[c, p, d - 1],
            ys.at[c, p, d - 1], yr.at[c, p, d - 1], along(1 - p, d),
        )

    def y_wait(c):
        for p in range(2):
            for d in (1, 3, 2):
                x_copy(c, p, d).wait_recv()

    def y_body(c):
        for p in range(2):
            total = t_part[c, rows_at(first_of(p) * 64, 64), cols_of(p)] + (
                x_recv[c, p, 0].astype(F32)
                + x_recv[c, p, 1].astype(F32)
                + x_recv[c, p, 2].astype(F32)
            )
            y_part[c, p] = total
            y_send[c, p] = total.astype(BF16)

    def y_start(c):
        for d in (2, 1, 3):
            for p in range(2):
                y_copy(c, p, d).start()
        c_copy(c).wait_send()
        for p in range(2):
            for d in (1, 2, 3):
                x_copy(c, p, d).wait_send()

    def y_gather(c, p, d):
        rows = rows_at(first_of(p) * 64 + second_of(p) * 16, 16)
        piece = g_out.at[c, rows, cols_of(p)]
        return remote(piece, piece, ys.at[c, p, 2 + d], yr.at[c, p, 2 + d], along(1 - p, d))

    def f_wait(c):
        for p in range(2):
            for d in (1, 2, 3):
                y_copy(c, p, d).wait_recv()

    def f_body(c):
        for p in range(2):
            mine = y_part[c, p, rows_at(second_of(p) * 16, 16), :]
            total = mine + (
                y_recv[c, p, 0].astype(F32)
                + y_recv[c, p, 1].astype(F32)
                + y_recv[c, p, 2].astype(F32)
            )
            rows = rows_at(first_of(p) * 64 + second_of(p) * 16, 16)
            g_out[c, rows, cols_of(p)] = total.astype(BF16)

    def f_start(c):
        for d in (2, 1, 3):
            for p in range(2):
                y_gather(c, p, d).start()
        for p in range(2):
            for d in (1, 2, 3):
                y_copy(c, p, d).wait_send()

    def a_copy(c, p, d):
        piece = g_out.at[c, rows_at(first_of(p) * 64, 64), cols_of(p)]
        return remote(
            piece, piece, ags.at[c, p, d - 1], agr.at[c, p, d - 1], along(p, d)
        )

    def out_rows(c):
        return pl.ds(pl.multiple_of(c * 512 + core * 256, 256), 256)

    def k_copy(c):
        return remote(g_out.at[c], gt_out.at[out_rows(c)], ks.at[c], kr.at[c], other)

    def l_copy(c):
        return pltpu.make_async_copy(g_out.at[c], gt_out.at[out_rows(c)], ls.at[c])

    def h_wait(c):
        for p in range(2):
            for d in (1, 2, 3):
                y_gather(c, p, d).wait_recv()

    def h_start(c):
        for d in (2, 1, 3):
            for p in range(2):
                a_copy(c, p, d).start()
        for p in range(2):
            for d in (1, 2, 3):
                y_gather(c, p, d).wait_send()

    def i_start(c):
        for p in range(2):
            for d in (1, 3, 2):
                a_copy(c, p, d).wait_recv()
        k_copy(c).start()
        l_copy(c).start()
        for p in range(2):
            for d in (1, 2, 3):
                a_copy(c, p, d).wait_send()

    def close(c):
        k_copy(c).wait()
        l_copy(c).wait()

    def nothing(_):
        pass

    ops = {
        "S": (nothing, None, nothing),
        "G": (nothing, lambda a: source_body(a, 1), source_start),
        "P": (nothing, lambda pair: source_body(2 * pair, 2), pair_start),
        "B": (second_wait, second_body, second_start),
        "C": (final_wait, final_body, final_start),
        "T": (nothing, target_body, target_start),
        "X": (x_wait, x_body, x_start),
        "Y": (y_wait, y_body, y_start),
        "F": (f_wait, f_body, f_start),
        "H": (h_wait, nothing, h_start),
        "I": (nothing, nothing, i_start),
    }
    for copy in loads[:5]:
        copy.wait()
    for index, block in enumerate(SCHEDULE):
        if index == 2:
            loads[5].wait()
        for op in block:
            ops[op[0]][0](int(op[1]))
        for op in block:
            if op[0] == "S":
                score(int(op[1]) * 2, 2, int(op[2]))
            else:
                ops[op[0]][1](int(op[1]))
        if index == 0:
            pl.semaphore_wait(barrier, len(peers))
        for op in block:
            ops[op[0]][2](int(op[1]))

    for c in range(4):
        close(c)
    for a in range(8):
        z_out_copy(a).wait()


def finish(gs_in, gt_in, gs_out, gt_out, gs_v, gt_v, in_sem, out_sem):
    pieces = []
    for n in range(8):
        rows = pl.ds(n * 256, 256)
        pieces.append((gt_in.at[rows], gt_v.at[rows], gt_out.at[rows]))
    for n in range(2):
        rows = pl.ds(n * 96, 96)
        pieces.append((gs_in.at[rows], gs_v.at[rows], gs_out.at[rows]))
    reads = [pltpu.make_async_copy(a, b, in_sem.at[n]) for n, (a, b, _) in enumerate(pieces)]
    writes = [pltpu.make_async_copy(b, c, out_sem.at[n]) for n, (_, b, c) in enumerate(pieces)]
    for copy in reads:
        copy.start()
    for read, write in zip(reads, writes):
        read.wait()
        write.start()
    for copy in writes:
        copy.wait()


def shards(
    source_embed, target_embed, source_potential, target_potential, active_blocks, active_count
):
    vmem = pl.BlockSpec(memory_space=pltpu.VMEM)
    smem = pl.BlockSpec(memory_space=pltpu.SMEM)
    hbm = pl.BlockSpec(memory_space=pl.ANY)
    dma = pltpu.SemaphoreType.DMA
    source_t, target = pl.pallas_call(
        kernel,
        out_shape=(
            jax.ShapeDtypeStruct((D // 4, ROWS), BF16),
            jax.ShapeDtypeStruct((ROWS, D), BF16),
        ),
        in_specs=[hbm, hbm, vmem, vmem, vmem, smem],
        out_specs=(hbm, hbm),
        scratch_shapes=[
            pltpu.VMEM((ROWS, D), BF16),
            pltpu.VMEM((ROWS, D), BF16),
            pltpu.VMEM((ROWS, ROWS), BF16),
            pltpu.VMEM((8, ROWS), F32),
            pltpu.VMEM((8, 4, 384, 128), F32),
            pltpu.VMEM((8, 2, 384, 128), BF16),
            pltpu.VMEM((8, 2, 384, 128), BF16),
            pltpu.VMEM((8, 2, 192, 128), BF16),
            pltpu.VMEM((8, 2, 192, 128), BF16),
            pltpu.VMEM((D // 4, ROWS), BF16),
            pltpu.VMEM((4, 256, D), F32),
            pltpu.VMEM((4, 256, D), BF16),
            pltpu.VMEM((4, 256, D), BF16),
            pltpu.VMEM((4, 2, 3, 64, 384), BF16),
            pltpu.VMEM((4, 2, 3, 64, 384), BF16),
            pltpu.VMEM((4, 2, 64, 384), F32),
            pltpu.VMEM((4, 2, 64, 384), BF16),
            pltpu.VMEM((4, 2, 3, 16, 384), BF16),
            pltpu.VMEM((4, 256, D), BF16),
            dma((6,)),
            dma((8, 4)),
            dma((8, 4)),
            dma((8,)),
            dma((4,)),
            dma((4,)),
            dma((4, 2, 3)),
            dma((4, 2, 3)),
            dma((4, 2, 6)),
            dma((4, 2, 6)),
            dma((4, 2, 3)),
            dma((4, 2, 3)),
            dma((4,)),
            dma((4,)),
            dma((4,)),
        ],
        compiler_params=pltpu.CompilerParams(
            collective_id=0, has_side_effects=True, vmem_limit_bytes=56 * 2**20
        ),
        cost_estimate=pl.CostEstimate(
            flops=3 * 2 * ROWS * ROWS * D, bytes_accessed=12 * 2**20, transcendentals=ROWS * ROWS
        ),
    )(
        source_embed,
        target_embed,
        source_potential.reshape(16, 128),
        target_potential.reshape(64, 128),
        active_blocks,
        active_count,
    )
    source_t, target = pl.pallas_call(
        finish,
        out_shape=(
            jax.ShapeDtypeStruct((D // 4, ROWS), BF16),
            jax.ShapeDtypeStruct((ROWS, D), BF16),
        ),
        in_specs=[hbm, hbm],
        out_specs=(hbm, hbm),
        scratch_shapes=[
            pltpu.VMEM((D // 4, ROWS), BF16),
            pltpu.VMEM((ROWS, D), BF16),
            dma((10,)),
            dma((10,)),
        ],
        compiler_params=pltpu.CompilerParams(vmem_limit_bytes=56 * 2**20),
    )(source_t, target)
    return source_t.T, target


def solution(mesh):
    return jax.shard_map(
        shards,
        mesh=mesh,
        in_specs=(P("src", None), P("tgt", None), P("src"), P(), P("src", None), P("src")),
        out_specs=(P("src", "tgt"), P("tgt", None)),
        check_vma=False,
    )
```

```python
import functools
import math

import jax
import jax.numpy as jnp
from jax import lax
from jax.experimental import pallas as pl
from jax.experimental.pallas import tpu as pltpu
from jax.sharding import PartitionSpec as P

D = 768
BLOCK = 256
ROWS = 2048
LAST = 3
LOG2E = 1.4426950408889634
SCALE = 2.0 / math.sqrt(D) * LOG2E
MESH = pl.DeviceIdType.MESH
F32 = jnp.float32
BF16 = jnp.bfloat16

SCHEDULE = (
    ("S00", "S01", "S02", "S03", "G0",),
    ("G1",),
    ("S10",),
    ("S11",),
    ("S12",),
    ("S13",),
    ("S20", "S30",),
    ("T0",),
    ("S21", "S31",),
    ("B0",),
    ("X0",),
    ("T1",),
    ("B1",),
    ("G2",),
    ("X1",),
    ("S22", "S32",),
    ("T2",),
    ("Y0",),
    ("G3",),
    ("X2",),
    ("S23", "S33",),
    ("T3",),
    ("Y1",),
    ("F0",),
    ("B2",),
    ("G4",),
    ("X3",),
    ("B3",),
    ("G5",),
    ("Y2",),
    ("F1",),
    ("H0",),
    ("G6",),
    ("G7",),
    ("B4",),
    ("F2",),
    ("Y3",),
    ("H1",),
    ("I0",),
    ("B5",),
    ("C0",),
    ("H2",),
    ("B6",),
    ("C1",),
    ("H3",),
    ("B7",),
    ("C2",),
    ("I1",),
    ("C3",),
    ("I2",),
    ("C4",),
    ("C5",),
    ("C6",),
    ("I3",),
    ("C7",),
)


def kernel(
    s_hbm, t_hbm, sp_ref, tp_ref, ids_ref, cnt_ref, gs_out, gt_out,
    s_v, t_v, plan, bias,
    z_part, z_send, z_recv, z2_send, z2_recv, z_out,
    t_part, c_send, c_recv, x_send, x_recv, y_part, y_send, y_recv, y_all, g_out,
    load_sem, zs, zr, zo, cs, cr, xs, xr, ys, yr, ags, agr, ls, ks, kr,
):
    src = lax.axis_index("src")
    z = lax.axis_index("tgt")
    x = src // 8
    y = (src // 2) % 4
    core = src % 2

    def at(x_, y_, core_, z_):
        return ((x_ * 4 + y_) * 2 + core_, z_)

    def along(path, step):
        if path == 0:
            return at((x + step) % 4, y, core, z)
        return at(x, (y + step) % 4, core, z)

    def along_z(step):
        return at(x, y, core, (z + step) % 4)

    other = at(x, y, 1 - core, z)
    peers = [along_z(1), along_z(3), other]
    peers += [along(p, d) for p in (0, 1) for d in (1, 2, 3)]

    barrier = pltpu.get_barrier_semaphore()
    for peer in peers:
        pl.semaphore_signal(barrier, inc=1, device_id=peer, device_id_type=MESH)

    def load(n, hbm_ref, ref, start, size):
        rows = pl.ds(start, size)
        return pltpu.make_async_copy(hbm_ref.at[rows], ref.at[rows], load_sem.at[n])

    loads = [load(0, s_hbm, s_v, 0, 512)]
    loads += [load(1 + n, t_hbm, t_v, n * 512, 512) for n in range(4)]
    loads += [load(5, s_hbm, s_v, 512, 1536)]
    for copy in loads:
        copy.start()

    sub = lax.broadcasted_iota(jnp.int32, (8, 24), 0)
    lane = lax.broadcasted_iota(jnp.int32, (8, 24), 1)
    count = jnp.zeros((8, 24), jnp.int32)
    for a in range(8):
        count = jnp.where(sub == a, cnt_ref[a], count)
    ids = jnp.where(lane < count, ids_ref[...], -1)
    tp = tp_ref[pl.ds(pl.multiple_of(z * 16, 16), 16), :] * LOG2E
    for b in range(8):
        hit = jnp.max(jnp.where(ids == z * 8 + b, 1.0, 0.0), axis=1, keepdims=True)
        for h in range(2):
            row = tp[2 * b + h:2 * b + h + 1, :]
            bias[:, b * 256 + h * 128:b * 256 + (h + 1) * 128] = jnp.where(
                hit > 0.5, row, -1e30
            )

    def remote(src_ref, dst_ref, send, recv, dev):
        return pltpu.make_async_remote_copy(
            src_ref=src_ref, dst_ref=dst_ref, send_sem=send, recv_sem=recv,
            device_id=dev, device_id_type=MESH,
        )

    def score(first, blocks, n):
        rows = blocks * BLOCK
        base = first * BLOCK
        cols = slice(n * 512, (n + 1) * 512)
        s = lax.dot_general(
            s_v[base:base + rows, :], t_v[cols, :], (((1,), (1,)), ((), ())),
            preferred_element_type=F32,
        )
        for i in range(blocks):
            tpr = bias[first + i:first + i + 1, cols]
            for h in range(2):
                q = 2 * i + h
                row = sp_ref[first * 2 + q:first * 2 + q + 1, :] * LOG2E
                pot = jnp.transpose(jnp.broadcast_to(row, (128, 128)))
                pot = jnp.concatenate([pot] * 4, axis=1)
                e = jnp.exp2(s[q * 128:(q + 1) * 128, :] * SCALE + (pot + tpr))
                plan[base + q * 128:base + (q + 1) * 128, cols] = e.astype(BF16)

    def z_copy(a, m):
        first, way = m < 2, m % 2
        return remote(
            z_send.at[a, way] if first else z2_send.at[a, way],
            z_recv.at[a, way] if first else z2_recv.at[a, way],
            zs.at[a, m], zr.at[a, m], along_z(1 if way == 0 else 3),
        )

    lane_low = lax.broadcasted_iota(jnp.int32, (128, 128), 1) < 64

    def source_body(first, blocks):
        base = first * BLOCK
        whole = jnp.dot(
            plan[base:base + blocks * BLOCK, :], t_v[...], preferred_element_type=F32
        )
        for i in range(blocks):
            a = first + i
            g = whole[i * BLOCK:(i + 1) * BLOCK, :]
            for o, tile in ((0, 0), (1, 2), (2, 3), (3, 5)):
                z_part[a, o, 0:256, :] = g[:, tile * 128:(tile + 1) * 128]
            for o, tile in ((0, 1), (2, 4)):
                top = g[0:128, tile * 128:(tile + 1) * 128]
                low = g[128:256, tile * 128:(tile + 1) * 128]
                z_part[a, o, 256:384, :] = jnp.where(lane_low, top, pltpu.roll(low, 64, 1))
                z_part[a, o + 1, 256:384, :] = jnp.where(lane_low, pltpu.roll(top, 64, 1), low)
            for way, half, o, r in ((0, 0, 2, 0), (0, 1, 1, 192), (1, 0, 2, 192), (1, 1, 3, 0)):
                z_send[a, way, half * 192:half * 192 + 192, :] = z_part[
                    a, (z + o) % 4, r:r + 192, :
                ].astype(BF16)

    def pair_start(pair):
        source_start(2 * pair)
        source_start(2 * pair + 1)

    def source_start(a):
        for m in (0, 1):
            z_copy(a, m).start()

    def second_wait(a):
        for m in (0, 1):
            z_copy(a, m).wait_recv()

    def second_body(a):
        for way, o, r in ((0, 1, 0), (1, 3, 192)):
            total = z_part[a, (z + o) % 4, r:r + 192, :] + z_recv[a, way, 0:192, :].astype(F32)
            z2_send[a, way] = total.astype(BF16)

    def second_start(a):
        for m in (2, 3):
            z_copy(a, m).start()

    def z_out_copy(a):
        cols = pl.ds(pl.multiple_of(a * BLOCK, BLOCK), BLOCK)
        return pltpu.make_async_copy(z_out.at[:, cols], gs_out.at[:, cols], zo.at[a])

    def final_wait(a):
        for m in (2, 3):
            z_copy(a, m).wait_recv()

    def final_body(a):
        first = z_part[a, z, 0:192, :] + (
            z2_recv[a, 0].astype(F32) + z_recv[a, 1, 192:384, :].astype(F32)
        )
        second = z_part[a, z, 192:384, :] + (
            z_recv[a, 0, 192:384, :].astype(F32) + z2_recv[a, 1].astype(F32)
        )
        whole = jnp.concatenate([first, second], axis=0)
        packed = whole[256:384, :]
        rolled = pltpu.roll(packed, 64, 1)
        odd = (z % 2) == 1
        for h in range(2):
            full = whole[h * 128:(h + 1) * 128, :]
            half = packed if h == 0 else rolled
            turned = pltpu.roll(full, 64, 1)
            left = jnp.where(odd, jnp.where(lane_low, half, turned), full)
            right = jnp.where(odd, turned, half)
            cols = pl.ds(pl.multiple_of(a * BLOCK + h * 128, 128), 128)
            z_out[0:128, cols] = jnp.transpose(left).astype(BF16)
            z_out[128:192, cols] = jnp.transpose(right)[0:64, :].astype(BF16)

    def final_start(a):
        z_out_copy(a).start()
        for m in range(4):
            z_copy(a, m).wait_send()

    def c_copy(c):
        return remote(c_send.at[c], c_recv.at[c], cs.at[c], cr.at[c], other)

    def target_body(c):
        cols = slice(c * 512, (c + 1) * 512)
        g = lax.dot_general(
            plan[:, cols], s_v[...], (((0,), (0,)), ((), ())), preferred_element_type=F32
        )
        low, high = g[0:256, :], g[256:512, :]
        t_part[c] = jnp.where(core == 0, low, high)
        c_send[c] = jnp.where(core == 0, high, low).astype(BF16)

    def target_start(c):
        c_copy(c).start()

    def x_copy(c, p, d):
        return remote(
            x_send.at[c, p, d - 1], x_recv.at[c, p, d - 1],
            xs.at[c, p, d - 1], xr.at[c, p, d - 1], along(p, d),
        )

    def first_of(p):
        return x if p == 0 else y

    def second_of(p):
        return y if p == 0 else x

    def cols_of(p):
        return slice(p * 384, (p + 1) * 384)

    def rows_at(start, size):
        return pl.ds(pl.multiple_of(start, 16), size)

    def x_wait(c):
        c_copy(c).wait_recv()

    def x_body(c):
        t_part[c] = t_part[c] + c_recv[c].astype(F32)
        for d in (1, 2, 3):
            for p in range(2):
                piece = (first_of(p) + d) % 4
                x_send[c, p, d - 1] = t_part[
                    c, rows_at(piece * 64, 64), cols_of(p)
                ].astype(BF16)

    def x_start(c):
        for d in (2, 1, 3):
            for p in range(2):
                x_copy(c, p, d).start()

    def y_copy(c, p, d):
        if c == LAST:
            mine = y_all.at[p, second_of(p)]
            return remote(
                mine, mine, ys.at[c, p, d - 1], yr.at[c, p, d - 1], along(1 - p, d)
            )
        piece = (second_of(p) + d) % 4
        return remote(
            y_send.at[c, p, rows_at(piece * 16, 16)], y_recv.at[c, p, d - 1],
            ys.at[c, p, d - 1], yr.at[c, p, d - 1], along(1 - p, d),
        )

    def y_wait(c):
        for p in range(2):
            for d in (1, 3, 2):
                x_copy(c, p, d).wait_recv()

    def y_body(c):
        for p in range(2):
            total = t_part[c, rows_at(first_of(p) * 64, 64), cols_of(p)] + (
                x_recv[c, p, 0].astype(F32)
                + x_recv[c, p, 1].astype(F32)
                + x_recv[c, p, 2].astype(F32)
            )
            if c == LAST:
                y_all[p, second_of(p)] = total.astype(BF16)
                continue
            y_part[c, p] = total
            y_send[c, p] = total.astype(BF16)

    def y_start(c):
        for d in (2, 1, 3):
            for p in range(2):
                y_copy(c, p, d).start()
        c_copy(c).wait_send()
        for p in range(2):
            for d in (1, 2, 3):
                x_copy(c, p, d).wait_send()

    def y_gather(c, p, d):
        rows = rows_at(first_of(p) * 64 + second_of(p) * 16, 16)
        piece = g_out.at[c, rows, cols_of(p)]
        return remote(piece, piece, ys.at[c, p, 2 + d], yr.at[c, p, 2 + d], along(1 - p, d))

    def f_wait(c):
        for p in range(2):
            for d in (1, 2, 3):
                y_copy(c, p, d).wait_recv()

    def f_body(c):
        for p in range(2):
            mine = y_part[c, p, rows_at(second_of(p) * 16, 16), :]
            total = mine + (
                y_recv[c, p, 0].astype(F32)
                + y_recv[c, p, 1].astype(F32)
                + y_recv[c, p, 2].astype(F32)
            )
            rows = rows_at(first_of(p) * 64 + second_of(p) * 16, 16)
            g_out[c, rows, cols_of(p)] = total.astype(BF16)

    def f_start(c):
        for d in (2, 1, 3):
            for p in range(2):
                y_gather(c, p, d).start()
        for p in range(2):
            for d in (1, 2, 3):
                y_copy(c, p, d).wait_send()

    def a_copy(c, p, d):
        piece = g_out.at[c, rows_at(first_of(p) * 64, 64), cols_of(p)]
        return remote(
            piece, piece, ags.at[c, p, d - 1], agr.at[c, p, d - 1], along(p, d)
        )

    def out_rows(c):
        return pl.ds(pl.multiple_of(c * 512 + core * 256, 256), 256)

    def k_copy(c):
        return remote(g_out.at[c], gt_out.at[out_rows(c)], ks.at[c], kr.at[c], other)

    def l_copy(c):
        return pltpu.make_async_copy(g_out.at[c], gt_out.at[out_rows(c)], ls.at[c])

    def h_wait(c):
        for p in range(2):
            for d in (1, 2, 3):
                (y_copy if c == LAST else y_gather)(c, p, d).wait_recv()

    def h_body(c):
        if c == LAST:
            for p in range(2):
                total = (
                    y_all[p, 0].astype(F32) + y_all[p, 1].astype(F32)
                    + y_all[p, 2].astype(F32) + y_all[p, 3].astype(F32)
                )
                g_out[c, rows_at(first_of(p) * 64, 64), cols_of(p)] = total.astype(BF16)

    def h_start(c):
        for d in (2, 1, 3):
            for p in range(2):
                a_copy(c, p, d).start()
        for p in range(2):
            for d in (1, 2, 3):
                (y_copy if c == LAST else y_gather)(c, p, d).wait_send()

    def i_start(c):
        for p in range(2):
            for d in (1, 3, 2):
                a_copy(c, p, d).wait_recv()
        k_copy(c).start()
        l_copy(c).start()
        for p in range(2):
            for d in (1, 2, 3):
                a_copy(c, p, d).wait_send()

    def close(c):
        k_copy(c).wait()
        l_copy(c).wait()

    def nothing(_):
        pass

    ops = {
        "S": (nothing, None, nothing),
        "G": (nothing, lambda a: source_body(a, 1), source_start),
        "P": (nothing, lambda pair: source_body(2 * pair, 2), pair_start),
        "B": (second_wait, second_body, second_start),
        "C": (final_wait, final_body, final_start),
        "T": (nothing, target_body, target_start),
        "X": (x_wait, x_body, x_start),
        "Y": (y_wait, y_body, y_start),
        "F": (f_wait, f_body, f_start),
        "H": (h_wait, h_body, h_start),
        "I": (nothing, nothing, i_start),
    }
    for copy in loads[:5]:
        copy.wait()
    for index, block in enumerate(SCHEDULE):
        if index == 2:
            loads[5].wait()
        for op in block:
            ops[op[0]][0](int(op[1]))
        for op in block:
            if op[0] == "S":
                score(int(op[1]) * 2, 2, int(op[2]))
            else:
                ops[op[0]][1](int(op[1]))
        if index == 0:
            pl.semaphore_wait(barrier, len(peers))
        for op in block:
            ops[op[0]][2](int(op[1]))

    for c in range(4):
        close(c)
    for a in range(8):
        z_out_copy(a).wait()


def finish(gs_in, gt_in, gs_out, gt_out, gs_v, gt_v, in_sem, out_sem):
    pieces = []
    for n in range(8):
        rows = pl.ds(n * 256, 256)
        pieces.append((gt_in.at[rows], gt_v.at[rows], gt_out.at[rows]))
    for n in range(2):
        rows = pl.ds(n * 96, 96)
        pieces.append((gs_in.at[rows], gs_v.at[rows], gs_out.at[rows]))
    reads = [pltpu.make_async_copy(a, b, in_sem.at[n]) for n, (a, b, _) in enumerate(pieces)]
    writes = [pltpu.make_async_copy(b, c, out_sem.at[n]) for n, (_, b, c) in enumerate(pieces)]
    for copy in reads:
        copy.start()
    for read, write in zip(reads, writes):
        read.wait()
        write.start()
    for copy in writes:
        copy.wait()


def shards(
    source_embed, target_embed, source_potential, target_potential, active_blocks, active_count
):
    vmem = pl.BlockSpec(memory_space=pltpu.VMEM)
    smem = pl.BlockSpec(memory_space=pltpu.SMEM)
    hbm = pl.BlockSpec(memory_space=pl.ANY)
    dma = pltpu.SemaphoreType.DMA
    source_t, target = pl.pallas_call(
        kernel,
        out_shape=(
            jax.ShapeDtypeStruct((D // 4, ROWS), BF16),
            jax.ShapeDtypeStruct((ROWS, D), BF16),
        ),
        in_specs=[hbm, hbm, vmem, vmem, vmem, smem],
        out_specs=(hbm, hbm),
        scratch_shapes=[
            pltpu.VMEM((ROWS, D), BF16),
            pltpu.VMEM((ROWS, D), BF16),
            pltpu.VMEM((ROWS, ROWS), BF16),
            pltpu.VMEM((8, ROWS), F32),
            pltpu.VMEM((8, 4, 384, 128), F32),
            pltpu.VMEM((8, 2, 384, 128), BF16),
            pltpu.VMEM((8, 2, 384, 128), BF16),
            pltpu.VMEM((8, 2, 192, 128), BF16),
            pltpu.VMEM((8, 2, 192, 128), BF16),
            pltpu.VMEM((D // 4, ROWS), BF16),
            pltpu.VMEM((4, 256, D), F32),
            pltpu.VMEM((4, 256, D), BF16),
            pltpu.VMEM((4, 256, D), BF16),
            pltpu.VMEM((4, 2, 3, 64, 384), BF16),
            pltpu.VMEM((4, 2, 3, 64, 384), BF16),
            pltpu.VMEM((4, 2, 64, 384), F32),
            pltpu.VMEM((4, 2, 64, 384), BF16),
            pltpu.VMEM((4, 2, 3, 16, 384), BF16),
            pltpu.VMEM((2, 4, 64, 384), BF16),
            pltpu.VMEM((4, 256, D), BF16),
            dma((6,)),
            dma((8, 4)),
            dma((8, 4)),
            dma((8,)),
            dma((4,)),
            dma((4,)),
            dma((4, 2, 3)),
            dma((4, 2, 3)),
            dma((4, 2, 6)),
            dma((4, 2, 6)),
            dma((4, 2, 3)),
            dma((4, 2, 3)),
            dma((4,)),
            dma((4,)),
            dma((4,)),
        ],
        compiler_params=pltpu.CompilerParams(
            collective_id=0, has_side_effects=True, vmem_limit_bytes=56 * 2**20
        ),
        cost_estimate=pl.CostEstimate(
            flops=3 * 2 * ROWS * ROWS * D, bytes_accessed=12 * 2**20, transcendentals=ROWS * ROWS
        ),
    )(
        source_embed,
        target_embed,
        source_potential.reshape(16, 128),
        target_potential.reshape(64, 128),
        active_blocks,
        active_count,
    )
    source_t, target = pl.pallas_call(
        finish,
        out_shape=(
            jax.ShapeDtypeStruct((D // 4, ROWS), BF16),
            jax.ShapeDtypeStruct((ROWS, D), BF16),
        ),
        in_specs=[hbm, hbm],
        out_specs=(hbm, hbm),
        scratch_shapes=[
            pltpu.VMEM((D // 4, ROWS), BF16),
            pltpu.VMEM((ROWS, D), BF16),
            dma((10,)),
            dma((10,)),
        ],
        compiler_params=pltpu.CompilerParams(vmem_limit_bytes=56 * 2**20),
    )(source_t, target)
    return source_t.T, target


def solution(mesh):
    return jax.shard_map(
        shards,
        mesh=mesh,
        in_specs=(P("src", None), P("tgt", None), P("src"), P(), P("src", None), P("src")),
        out_specs=(P("src", "tgt"), P("tgt", None)),
        check_vma=False,
    )
```
